256 devices in a mesh: span: 8 (over x, y_lo), tile: 32 (over z, y_hi, core).
Axes of the slice: x: 4, y: 4 (y_hi: 2, y_lo: 2; y = y_hi * 2 + y_lo), z: 8, core: 2. Of those that a mesh axis runs over, the one named last changes fastest.
Arguments:
- tokens: bfloat16 [8, 2304, 1536], P('span', 'tile'), may hold values from -6 to 6
- noise_steps: int32 [8], replicated, may hold values from 0 to 7, as said below
- span_mask: int32 [8, 8], replicated, may hold values from 0 to 1, as said below
- modulation: float32 [8, 5, 1536], replicated, may hold values from -3 to 3
- qkv_weight: bfloat16 [768, 9216], P(None, 'span'), may hold values from -1.5 to 1.5
- out_weight: bfloat16 [1536, 1536], P('span'), may hold values from -0.15625 to 0.15625
- head_weight: bfloat16 [768, 128], replicated, may hold values from -0.15625 to 0.15625
- head_bias: float32 [64], replicated, may hold values from -3 to 3
- frame_cache: bfloat16 [2, 64, 48, 16], P(None, 'tile'), may hold values from -6 to 6
- conv_weight: bfloat16 [432, 384], replicated, may hold values from -0.3125 to 0.3125
- conv_bias: float32 [384], replicated, may hold values from -3 to 3
Outputs:
- hidden_out: bfloat16 [8, 2304, 1536], P('span', 'tile')
- decoded_frames: bfloat16 [3, 64, 48, 384], P(None, 'tile', 'span')
The draws below stay inside these ranges and needn't reach their ends.
Inputs may be any that keep to these rules, and one draw needn't show every extreme that they name: `noise_steps`: span 0, the finishing span, has level 0 and span 8 - 1 has level 7; the others lie in 1 to 7. `span_mask`: 1 on the diagonal, 0 above it, 0 or 1 below it.
All inputs are finite; a program needn't handle non-finite values.
Results may differ from the reference program's by a relative error of at most 0.015.
Values may be sent and summed in bfloat16 or wider, within the bound.
No kernel may reach another device: no remote copies, remote signals or barrier semaphores. Data moves between devices by JAX's collectives and lax.ppermute only.
A program may use at most 128 MiB of HBM per device.

```python
import jax
import jax.numpy as jnp
from jax import lax

D = 1536
HEADS = 24
HDIM = 64
LCH = 16
VCH = 384
LEVELS = 8
LF = 3
TROW_DEV = 1
TCOL = 24
SPANS = 8
TOKENS = 2304
LROWS = 64
LW = 48
N_TILE = 32


def draw_noise_steps(key, part):
    middle = jax.random.randint(key, (SPANS,), 1, LEVELS)
    place = jnp.arange(SPANS)
    return jnp.where(place == 0, 0, jnp.where(place == SPANS - 1, LEVELS - 1, middle)).astype(jnp.int32)


def draw_span_mask(key, part):
    coins = jax.random.randint(key, (SPANS, SPANS), 0, 2)
    row_index = jnp.arange(SPANS)[:, None]
    col_index = jnp.arange(SPANS)[None, :]
    return jnp.where(row_index == col_index, 1, jnp.where(col_index < row_index, coins, 0)).astype(jnp.int32)


def draw_tokens(key, part):
    base = jax.random.truncated_normal(jax.random.fold_in(key, 1), -6.0, 6.0, (SPANS, TOKENS, D), jnp.float32)
    return base.astype(jnp.bfloat16)


def draw_qkv_weight(key, part):
    half_rows = D // 2
    drawn = jax.random.truncated_normal(jax.random.fold_in(key, 21), -6.0, 6.0, (half_rows, HEADS, 2, 3, HDIM), jnp.float32)
    weights_out = drawn * D ** (-0.5)
    return weights_out.reshape(half_rows, 6 * D).astype(jnp.bfloat16)


def block_scale(rng, shape, cuts, least, high):
    def one(dim, parts):
        steps = jax.random.uniform(jax.random.fold_in(jax.random.fold_in(rng, 6), dim), (parts,), jnp.float32, least / len(cuts), high / len(cuts))
        return jnp.repeat(jnp.exp(steps), shape[dim] // parts).reshape((-1,) + (1,) * (len(shape) - dim - 1))

    factor_of = one(*cuts[0])
    for cut in cuts[1:]:
        factor_of = factor_of * one(*cut)
    return factor_of


def bell_draw(own_key, extent, scale, limit, shards=(), dtype=jnp.bfloat16):
    values = scale * jax.random.normal(own_key, extent, jnp.float32)
    if shards:
        values = values * block_scale(own_key, extent, shards, -0.22, 0.18)
    return jnp.clip(values, -limit, limit).astype(dtype)


def setup_inputs(seed: int = 0) -> dict:
    streams_of = jax.random.split(jax.random.key(seed), 12)
    tokens = draw_tokens(jax.random.fold_in(streams_of[11], 71), 0)
    noise_steps = draw_noise_steps(jax.random.fold_in(streams_of[11], 71), 0)
    span_mask = draw_span_mask(jax.random.fold_in(streams_of[11], 71), 0)
    modulation = bell_draw(streams_of[3], (LEVELS, 5, D), 0.5, 3.0, (), jnp.float32)
    qkv_weight = draw_qkv_weight(jax.random.fold_in(streams_of[11], 71), 0)
    out_weight = bell_draw(streams_of[5], (D, D), D ** -0.5, 0.15625, ((0, 8),))
    head_weight = bell_draw(streams_of[6], (D // 2, 8 * LCH), D ** -0.5, 0.15625)
    head_bias = bell_draw(streams_of[7], (4 * LCH,), 0.5, 3.0, (), jnp.float32)
    frame_cache = bell_draw(streams_of[8], (2, LROWS, LW, LCH), 1.0, 6.0, ((1, 32),))
    conv_weight = bell_draw(streams_of[9], (27 * LCH, VCH), (27 * LCH) ** -0.5, 0.3125)
    conv_bias = bell_draw(streams_of[10], (VCH,), 0.5, 3.0, (), jnp.float32)
    return {"tokens": tokens, "noise_steps": noise_steps, "span_mask": span_mask, "modulation": modulation, "qkv_weight": qkv_weight, "out_weight": out_weight, "head_weight": head_weight, "head_bias": head_bias, "frame_cache": frame_cache, "conv_weight": conv_weight, "conv_bias": conv_bias}


epsilon = 1e-06
masked_score = -1e+30

def layer_norm(values):
    centred = values - lax.optimization_barrier(jnp.mean(values, axis=-1, keepdims=True))
    spread = lax.optimization_barrier(jnp.mean(centred * centred, axis=-1, keepdims=True))
    return centred * lax.rsqrt(spread + epsilon)

def convolve(padded, kernel, offsets, frame_count, row_count, col_count):
    pieces = []
    for frame_step in range(3):
        for row_step in range(3):
            for col_step in range(3):
                pieces.append(padded[frame_step:frame_step + frame_count, row_step:row_step + row_count, col_step:col_step + col_count])
    stacked = jnp.concatenate(pieces, axis=-1)
    product = jnp.dot(stacked.reshape(-1, stacked.shape[-1]), kernel, preferred_element_type=jnp.float32)
    return (product.reshape(frame_count, row_count, col_count, -1) + offsets).astype(jnp.bfloat16)

def reference(tokens, noise_steps, span_mask, modulation, qkv_weight, out_weight, head_weight, head_bias, frame_cache, conv_weight, conv_bias):
    mods = modulation[noise_steps]
    residual = tokens.astype(jnp.float32)
    normed = (layer_norm(residual) * (1.0 + mods[:, 1][:, None]) + mods[:, 0][:, None]).astype(jnp.bfloat16)
    full_weight = jnp.transpose(qkv_weight.reshape(D // 2, HEADS, 2, 3, HDIM), (0, 2, 3, 1, 4)).reshape(D, 3 * D)
    projected = jnp.dot(normed.reshape(-1, D), full_weight, preferred_element_type=jnp.float32).astype(jnp.bfloat16)
    projected = projected.reshape(SPANS, TOKENS, 3, HEADS, HDIM)
    queries = jnp.transpose(projected[:, :, 0], (0, 2, 1, 3))
    key_rows = jnp.transpose(projected[:, :, 1].reshape(SPANS * TOKENS, HEADS, HDIM), (1, 0, 2))
    value_rows = jnp.transpose(projected[:, :, 2].reshape(SPANS * TOKENS, HEADS, HDIM), (1, 0, 2))
    visible = jnp.repeat(span_mask > 0, TOKENS, axis=1)
    score_scale = HDIM ** (-0.5)

    def per_span(inputs):
        span_queries, seen = inputs

        def per_head(head_inputs):
            head_queries, head_keys, head_values = head_inputs
            scores = jnp.dot(head_queries, head_keys.T, preferred_element_type=jnp.float32) * score_scale
            scores = jnp.where(seen[None, :], scores, masked_score)
            largest = lax.optimization_barrier(jnp.max(scores, axis=-1, keepdims=True))
            probs = jnp.where(seen[None, :], jnp.exp(scores - largest), 0.0)
            row_total = lax.optimization_barrier(jnp.sum(probs, axis=-1, keepdims=True))
            blended = jnp.dot(probs.astype(jnp.bfloat16), head_values, preferred_element_type=jnp.float32)
            return (blended / row_total).astype(jnp.bfloat16)
        return lax.map(per_head, (span_queries, key_rows, value_rows))
    attended = lax.map(per_span, (queries, visible))
    merged = jnp.transpose(attended, (0, 2, 1, 3)).reshape(SPANS * TOKENS, D)
    projected_out = jnp.dot(merged, out_weight, preferred_element_type=jnp.float32).reshape(SPANS, TOKENS, D)
    hidden_out = (residual + mods[:, 2][:, None] * projected_out).astype(jnp.bfloat16)
    finished = hidden_out[0].astype(jnp.float32)
    shaped = (layer_norm(finished) * (1.0 + mods[0, 4]) + mods[0, 3]).astype(jnp.bfloat16)
    head_full = head_weight.reshape(D, 4 * LCH)
    patches = (jnp.dot(shaped, head_full, preferred_element_type=jnp.float32) + head_bias).astype(jnp.bfloat16)
    latent = patches.reshape(N_TILE, LF, TROW_DEV, TCOL, 2, 2, LCH)
    latent = jnp.transpose(latent, (1, 0, 2, 4, 3, 5, 6)).reshape(LF, LROWS, LW, LCH)
    frames = jnp.concatenate([frame_cache, latent], axis=0)
    padded = jnp.pad(frames, ((0, 0), (1, 1), (1, 1), (0, 0)))
    decoded_frames = convolve(padded, conv_weight, conv_bias, LF, LROWS, LW)
    return (hidden_out, decoded_frames)
```

```python
import functools

import jax
import jax.numpy as jnp
from jax import lax
from jax.experimental import pallas as pl
from jax.experimental.pallas import tpu as pltpu
from jax.sharding import Mesh
from jax.sharding import PartitionSpec as P

HDIM = 64
LCH = 16
LF = 3
TCOL = 24
D = 1536
SPANS = 8
ROWS = 72
VCH = 384
GROUP = 3
LANES = 256
KVW = 384
EPS = 1e-06
LOW = -1e30
SPAN = ("x", "ylo")
TILE = ("z", "yhi", "core")
VMEM_LIMIT = 48 * 1024 * 1024

bf16 = jnp.bfloat16
f32 = jnp.float32


def shift(block, axis, count, step):
    return lax.ppermute(block, axis, [(i, (i + step) % count) for i in range(count)])


def normalise(values):
    centred = values - jnp.mean(values, axis=-1, keepdims=True)
    spread = jnp.mean(centred * centred, axis=-1, keepdims=True)
    return centred * lax.rsqrt(spread + EPS)


def qkv_kernel(place, levels, mod, perm, weight, *refs):
    tokens = refs[:SPANS]
    q_ref, kv_ref, normed = refs[SPANS:]
    me = place[0]
    for step in range(SPANS):
        span = lax.rem(me - step + SPANS, SPANS)
        level = levels[span]
        values = normalise(tokens[step][...].astype(f32))
        values = values * (1.0 + mod[level, 1:2, :]) + mod[level, 0:1, :]
        normed[step * ROWS : (step + 1) * ROWS, :] = values
    total = jnp.zeros((SPANS * ROWS, LANES + KVW), f32)
    for block in range(D // 256):
        part = normed[:, block * 256 : (block + 1) * 256].astype(bf16)
        part = jnp.dot(part, perm[...], preferred_element_type=f32).astype(bf16)
        total += jnp.dot(
            part, weight[block * 256 : (block + 1) * 256, :], preferred_element_type=f32
        )
    for step in range(SPANS):
        span = lax.rem(me - step + SPANS, SPANS)
        rows = total[step * ROWS : (step + 1) * ROWS, :].astype(bf16)
        q_ref[span] = rows[:, :LANES] * jnp.asarray(HDIM**-0.5, bf16)
        kv_ref[span] = rows[:, LANES:]


def arrange_kernel(raw, out):
    width = LANES + KVW
    row = lax.broadcasted_iota(jnp.int32, (256, width), 0)
    col = lax.broadcasted_iota(jnp.int32, (256, width), 1) - HDIM
    kind = col // (GROUP * HDIM)
    head = (col % (GROUP * HDIM)) // HDIM
    source = jnp.where(kind == 0, 0, 3 - kind) * HDIM + col % HDIM
    for parity in range(2):
        total = jnp.zeros((D // 2, width), f32)
        for group in range(GROUP):
            begin = group * 2 * KVW // 2 + parity * 128
            wanted = (row == source + parity * HDIM) & (head == group) & (col >= 0)
            total += jnp.dot(
                raw[:, begin : begin + 256],
                jnp.where(wanted, 1.0, 0.0).astype(bf16),
                preferred_element_type=f32,
            )
        for block in range(D // 256):
            out[block * 256 + parity * 128 : block * 256 + parity * 128 + 128, :] = total[
                block * 128 : (block + 1) * 128
            ].astype(bf16)


def arrange(raw):
    vmem = pl.BlockSpec(memory_space=pltpu.VMEM)
    return pl.pallas_call(
        arrange_kernel,
        out_shape=jax.ShapeDtypeStruct((D, LANES + KVW), bf16),
        in_specs=[vmem],
        out_specs=vmem,
        compiler_params=pltpu.CompilerParams(vmem_limit_bytes=VMEM_LIMIT),
        cost_estimate=pl.CostEstimate(
            flops=4000000000, bytes_accessed=4000000, transcendentals=0
        ),
        name="arrange",
    )(raw)


def project_spans(place, levels, modulation, weight, blocks):
    row = jnp.arange(256)
    perm = (row[:, None] == (2 * (row % 128) + row // 128)[None, :]).astype(bf16)
    smem = pl.BlockSpec(memory_space=pltpu.SMEM)
    vmem = pl.BlockSpec(memory_space=pltpu.VMEM)
    return pl.pallas_call(
        qkv_kernel,
        out_shape=(
            jax.ShapeDtypeStruct((SPANS, ROWS, LANES), bf16),
            jax.ShapeDtypeStruct((SPANS, ROWS, KVW), bf16),
        ),
        in_specs=[smem, smem] + [vmem] * (3 + SPANS),
        out_specs=(vmem, vmem),
        scratch_shapes=[pltpu.VMEM((SPANS * ROWS, D), f32)],
        compiler_params=pltpu.CompilerParams(vmem_limit_bytes=VMEM_LIMIT),
        cost_estimate=pl.CostEstimate(
            flops=2 * SPANS * ROWS * D * 640, bytes_accessed=4500000, transcendentals=0
        ),
        name="qkv",
    )(place, levels, modulation, perm, weight, *blocks)


def split_bf16(value, count):
    parts = []
    for _ in range(count):
        part = value.astype(bf16).astype(f32)
        parts.append(part)
        value = value - part
    return parts


def attend_kernel(
    place, mask, qa, qb, kv, out, pairs, queries, keys, values, s0, s1, p0, p1, r0, r1, acc, peak
):
    step = pl.program_id(0)
    count = kv.shape[0] * ROWS
    rows = 2 * ROWS
    stack = GROUP * rows
    lane = lax.broadcasted_iota(jnp.int32, (1, LANES), 1)

    @pl.when(step == 0)
    def _():
        for span in range(SPANS):
            both = jnp.concatenate([qa[span].astype(f32), qb[span].astype(f32)], axis=0)
            for head in range(GROUP):
                queries[span, head * rows : (head + 1) * rows, :] = jnp.where(
                    lane // HDIM == head + 1, both, 0.0
                ).astype(bf16)
        queries[SPANS] = jnp.zeros((stack, LANES), bf16)
        acc[...] = jnp.zeros_like(acc)
        peak[...] = jnp.full_like(peak, LOW)
        p0[...] = jnp.zeros_like(p0)
        r0[...] = jnp.zeros_like(r0)

    block = kv[:, 0].astype(f32).reshape(count, KVW)
    values[step] = jnp.where(lane // HDIM == 3, 1.0, block[:, :LANES]).astype(bf16)
    keys[step] = block[:, KVW - LANES :].astype(bf16)

    def put(index, span, key_span):
        pairs[2 * index] = span
        pairs[2 * index + 1] = key_span

    def score(index, scores):
        scores[...] = lax.dot_general(
            queries[pairs[2 * index]],
            keys[pairs[2 * index + 1]],
            (((1,), (1,)), ((), ())),
            preferred_element_type=f32,
        )

    def weigh(index, scores, probs, rescale):
        span = pairs[2 * index]
        old = peak[span, :, 0:1]
        block = scores[...]
        new = jnp.maximum(old, jnp.max(block, axis=1, keepdims=True))
        probs[...] = jnp.exp(block - new).astype(bf16)
        peak[span] = jnp.broadcast_to(new, (stack, 128))
        rescale[...] = jnp.broadcast_to(jnp.exp(old - new), (stack, 128))

    def blend(index, probs, rescale):
        span = pairs[2 * index]
        acc[span] = acc[span] * rescale[:, 0:1] + jnp.dot(
            probs[...], values[pairs[2 * index + 1]], preferred_element_type=f32
        )

    @pl.when(step == SPANS - 1)
    def _():
        put(0, SPANS, 0)

        def scan(at, found):
            span, key_span = at // SPANS, at % SPANS
            seen = mask[span, key_span] > 0

            @pl.when(seen)
            def _():
                put(found, span, key_span)

            return jnp.where(seen, found + 1, found)

        found = lax.fori_loop(0, SPANS * SPANS, scan, jnp.int32(1))
        for extra in range(4):
            put(found + extra, SPANS, 0)
        score(1, s1)

        def both_slots(trip, carry):
            at = 2 * trip + 1
            score(at + 1, s0)
            weigh(at, s1, p1, r1)
            blend(at - 1, p0, r0)
            score(at + 2, s1)
            weigh(at + 1, s0, p0, r0)
            blend(at, p1, r1)
            return carry

        lax.fori_loop(0, (found + 1) // 2, both_slots, 0)

        mine = place[1]
        for span in range(SPANS):
            heads = [acc[span, head * rows : (head + 1) * rows, :] for head in range(GROUP)]
            merged = jnp.where(lane < HDIM, heads[0], jnp.where(lane < 2 * HDIM, heads[1], heads[2]))
            columns = []
            for head in range(GROUP):
                columns += split_bf16(peak[span, head * rows : (head + 1) * rows, 0:1], 3)
                columns += split_bf16(heads[head][:, 192:193], 2)
            for index, column in enumerate(columns):
                merged = jnp.where(lane == 192 + index, column, merged)
            out[span, mine] = merged[:ROWS].astype(bf16)
            out[span, 1 - mine] = merged[ROWS:].astype(bf16)


def attend(place, mask, qa, qb, kv):
    sources = kv.shape[0]
    smem = pl.BlockSpec(memory_space=pltpu.SMEM)
    vmem = pl.BlockSpec(memory_space=pltpu.VMEM)
    stack = 2 * ROWS * GROUP
    count = sources * ROWS
    return pl.pallas_call(
        attend_kernel,
        grid=(SPANS,),
        out_shape=jax.ShapeDtypeStruct((SPANS, 2, ROWS, LANES), bf16),
        in_specs=[
            smem,
            smem,
            vmem,
            vmem,
            pl.BlockSpec((sources, 1, ROWS, KVW), lambda i: (0, i, 0, 0)),
        ],
        out_specs=pl.BlockSpec((SPANS, 2, ROWS, LANES), lambda i: (0, 0, 0, 0)),
        scratch_shapes=[
            pltpu.SMEM((2 * (SPANS * SPANS + 8),), jnp.int32),
            pltpu.VMEM((SPANS + 1, stack, LANES), bf16),
            pltpu.VMEM((SPANS, count, LANES), bf16),
            pltpu.VMEM((SPANS, count, LANES), bf16),
            pltpu.VMEM((stack, count), f32),
            pltpu.VMEM((stack, count), f32),
            pltpu.VMEM((stack, count), bf16),
            pltpu.VMEM((stack, count), bf16),
            pltpu.VMEM((stack, 128), f32),
            pltpu.VMEM((stack, 128), f32),
            pltpu.VMEM((SPANS + 1, stack, LANES), f32),
            pltpu.VMEM((SPANS + 1, stack, 128), f32),
        ],
        compiler_params=pltpu.CompilerParams(
            vmem_limit_bytes=VMEM_LIMIT, dimension_semantics=("arbitrary",)
        ),
        cost_estimate=pl.CostEstimate(
            flops=8000000000, bytes_accessed=8000000, transcendentals=12000000
        ),
        name="attend",
    )(place, mask, qa, qb, kv)


def finish_kernel(
    place, levels, parts, near, far, tokens, mod, head_full, bias, hidden, patches, weight
):
    lane = lax.broadcasted_iota(jnp.int32, (HDIM, LANES), 1)
    slot = lax.broadcasted_iota(jnp.int32, (HDIM, LANES), 0)
    head = lane // HDIM
    peaks = jnp.where((slot >= head * 5) & (slot < head * 5 + 3) & (head < 3), 1.0, 0.0).astype(bf16)
    sums = jnp.where((slot >= head * 5 + 3) & (slot < head * 5 + 5) & (head < 3), 1.0, 0.0).astype(
        bf16
    )
    total = jnp.zeros((ROWS, D), f32)
    core = place[2]
    for step in range(SPANS):
        group = lax.rem(place[0] - step + SPANS, SPANS)
        weight[:96, :] = jnp.where(core == 0, near[step], far[step])
        weight[96:, :] = jnp.where(core == 0, far[step], near[step])
        tops, totals, outs = [], [], []
        for half in range(2):
            part = parts[group * 2 + half]
            tops.append(jnp.dot(part[:, 192:], peaks, preferred_element_type=f32))
            totals.append(jnp.dot(part[:, 192:], sums, preferred_element_type=f32))
            outs.append(part.astype(f32))
        top = jnp.maximum(tops[0], tops[1])
        scale = [jnp.exp(tops[0] - top), jnp.exp(tops[1] - top)]
        blended = (outs[0] * scale[0] + outs[1] * scale[1]) / (
            totals[0] * scale[0] + totals[1] * scale[1]
        )
        total += jnp.dot(
            blended[:, :192].astype(bf16),
            weight[...],
            preferred_element_type=f32,
        )
    level = levels[place[0]]
    result = (tokens[...].astype(f32) + mod[level, 2:3, :] * total).astype(bf16)
    hidden[...] = result
    first = levels[0]
    shaped = normalise(result.astype(f32)) * (1.0 + mod[first, 4:5, :]) + mod[first, 3:4, :]
    patches[...] = (
        jnp.dot(shaped.astype(bf16), head_full[...], preferred_element_type=f32) + bias[...]
    ).astype(bf16)


def finish(place, levels, parts, near, far, tokens, modulation, head_full, bias):
    smem = pl.BlockSpec(memory_space=pltpu.SMEM)
    vmem = pl.BlockSpec(memory_space=pltpu.VMEM)
    return pl.pallas_call(
        finish_kernel,
        out_shape=(
            jax.ShapeDtypeStruct((ROWS, D), bf16),
            jax.ShapeDtypeStruct((ROWS, 4 * LCH), bf16),
        ),
        in_specs=[smem, smem] + [vmem] * 7,
        out_specs=(vmem, vmem),
        scratch_shapes=[pltpu.VMEM((192, D), bf16)],
        compiler_params=pltpu.CompilerParams(vmem_limit_bytes=VMEM_LIMIT),
        cost_estimate=pl.CostEstimate(
            flops=2 * ROWS * D * D, bytes_accessed=6000000, transcendentals=0
        ),
        name="finish",
    )(place, levels, parts, near, far, tokens, modulation, head_full, bias)


def per_device(
    tokens,
    noise_steps,
    span_mask,
    modulation,
    qkv_weight,
    out_weight,
    head_weight,
    head_bias,
    frame_cache,
    conv_weight,
    conv_bias,
):
    span = lax.axis_index(SPAN)
    yhi = lax.axis_index("yhi")
    core = lax.axis_index("core")
    place = jnp.stack([span, yhi, core]).astype(jnp.int32)
    own = tokens[0]

    blocks = [own] + [shift(own, SPAN, SPANS, step) for step in range(1, SPANS)]

    weight = arrange(qkv_weight)
    q_own, kv_own = project_spans(place, noise_steps, modulation, weight, blocks)

    kv = lax.all_gather(kv_own, ("z", "core"))
    q_other = shift(q_own, "yhi", 2, 1)

    half = lax.dynamic_slice_in_dim(out_weight, core * 96, 96, 0)
    half, _ = lax.optimization_barrier((half, q_own))
    halves = [half] + [shift(half, SPAN, SPANS, step) for step in range(1, SPANS)]
    stacked = jnp.stack(halves)
    other = shift(stacked, "core", 2, 1)
    partial = attend(place, span_mask, q_own, q_other, kv)
    parts = lax.all_to_all(
        partial.reshape(2 * SPANS, ROWS, LANES), SPAN + ("yhi",), 0, 0
    )
    hidden, patches = finish(
        place,
        noise_steps,
        parts,
        stacked,
        other,
        own,
        modulation,
        head_weight.reshape(D, 4 * LCH),
        head_bias[None, :],
    )

    spread = lax.all_to_all(jnp.broadcast_to(patches[None], (SPANS,) + patches.shape), SPAN, 0, 0)
    latent = spread[0].reshape(LF, TCOL, 2, 2, LCH)
    latent = jnp.transpose(latent, (0, 2, 1, 3, 4)).reshape(LF, 2, 2 * TCOL, LCH)
    frames = jnp.concatenate([frame_cache, latent], axis=0)
    up = [(i, i + 1) for i in range(31)]
    down = [(i + 1, i) for i in range(31)]
    above = lax.ppermute(frames[:, 1:2], TILE, up)
    below = lax.ppermute(frames[:, 0:1], TILE, down)
    padded = jnp.concatenate([above, frames, below], axis=1)
    padded = jnp.pad(padded, ((0, 0), (0, 0), (1, 1), (0, 0)))
    mine = lax.dynamic_slice_in_dim(padded, span * 6, 8, axis=2)
    pieces = []
    for a in range(3):
        for b in range(3):
            for e in range(3):
                pieces.append(mine[a : a + 3, b : b + 2, e : e + 6])
    cells = jnp.concatenate(pieces, axis=-1).reshape(36, 27 * LCH)
    product = jnp.dot(cells, conv_weight, preferred_element_type=f32) + conv_bias
    decoded = product.astype(bf16).reshape(3, 2, 6, VCH)
    return (hidden[None], decoded)


def solution(mesh):
    fine = Mesh(mesh.devices.reshape(4, 2, 8, 2, 2), SPAN + TILE)
    in_specs = (
        P(SPAN, TILE, None),
        P(),
        P(),
        P(),
        P(None, SPAN),
        P(SPAN, None),
        P(),
        P(),
        P(None, TILE, None, None),
        P(),
        P(),
    )
    out_specs = (P(SPAN, TILE, None), P(None, TILE, SPAN, None))
    return jax.shard_map(
        per_device, mesh=fine, in_specs=in_specs, out_specs=out_specs, check_vma=False
    )
```

```python
import functools

import jax
import jax.numpy as jnp
from jax import lax
from jax.experimental import pallas as pl
from jax.experimental.pallas import tpu as pltpu
from jax.sharding import Mesh
from jax.sharding import PartitionSpec as P

HDIM = 64
LCH = 16
LF = 3
TCOL = 24
D = 1536
SPANS = 8
ROWS = 72
VCH = 384
GROUP = 3
LANES = 256
KVW = 384
EPS = 1e-06
LOW = -1e30
SPAN = ("x", "ylo")
TILE = ("z", "yhi", "core")
VMEM_LIMIT = 48 * 1024 * 1024
OFFSETS = ((0, 0), (0, 1), (3, 0), (1, 0), (3, 1), (1, 1), (2, 0), (2, 1))

bf16 = jnp.bfloat16
f32 = jnp.float32


def shift(block, axis, count, step):
    return lax.ppermute(block, axis, [(i, (i + step) % count) for i in range(count)])


def normalise(values):
    centred = values - jnp.mean(values, axis=-1, keepdims=True)
    spread = jnp.mean(centred * centred, axis=-1, keepdims=True)
    return centred * lax.rsqrt(spread + EPS)


def qkv_kernel(place, levels, mod, perm, weight, *refs):
    tokens = refs[:SPANS]
    q_ref, kv_ref, first_ref, normed = refs[SPANS:]
    me = place[0]
    for step in range(SPANS):
        span = lax.rem(me // 2 + OFFSETS[step][0], 4) * 2 + lax.rem(me + OFFSETS[step][1], 2)
        level = levels[span]
        values = normalise(tokens[step][...].astype(f32))
        values = values * (1.0 + mod[level, 1:2, :]) + mod[level, 0:1, :]
        normed[step * ROWS : (step + 1) * ROWS, :] = values
    total = jnp.zeros((SPANS * ROWS, LANES + KVW), f32)
    for block in range(D // 256):
        part = normed[:, block * 256 : (block + 1) * 256].astype(bf16)
        part = jnp.dot(part, perm[...], preferred_element_type=f32).astype(bf16)
        total += jnp.dot(
            part, weight[block * 256 : (block + 1) * 256, :], preferred_element_type=f32
        )
    for step in range(SPANS):
        span = lax.rem(me // 2 + OFFSETS[step][0], 4) * 2 + lax.rem(me + OFFSETS[step][1], 2)
        rows = total[step * ROWS : (step + 1) * ROWS, :].astype(bf16)
        q_ref[span] = rows[:, :LANES] * jnp.asarray(HDIM**-0.5, bf16)
        kv_ref[span] = rows[:, LANES:]

        @pl.when(span == 0)
        def _():
            first_ref[...] = tokens[step][...]


def arrange_kernel(raw, out):
    width = LANES + KVW
    row = lax.broadcasted_iota(jnp.int32, (256, width), 0)
    col = lax.broadcasted_iota(jnp.int32, (256, width), 1) - HDIM
    kind = col // (GROUP * HDIM)
    head = (col % (GROUP * HDIM)) // HDIM
    source = jnp.where(kind == 0, 0, 3 - kind) * HDIM + col % HDIM
    for parity in range(2):
        total = jnp.zeros((D // 2, width), f32)
        for group in range(GROUP):
            begin = group * 2 * KVW // 2 + parity * 128
            wanted = (row == source + parity * HDIM) & (head == group) & (col >= 0)
            total += jnp.dot(
                raw[:, begin : begin + 256],
                jnp.where(wanted, 1.0, 0.0).astype(bf16),
                preferred_element_type=f32,
            )
        for block in range(D // 256):
            out[block * 256 + parity * 128 : block * 256 + parity * 128 + 128, :] = total[
                block * 128 : (block + 1) * 128
            ].astype(bf16)


def arrange(raw):
    vmem = pl.BlockSpec(memory_space=pltpu.VMEM)
    return pl.pallas_call(
        arrange_kernel,
        out_shape=jax.ShapeDtypeStruct((D, LANES + KVW), bf16),
        in_specs=[vmem],
        out_specs=vmem,
        compiler_params=pltpu.CompilerParams(vmem_limit_bytes=VMEM_LIMIT),
        cost_estimate=pl.CostEstimate(
            flops=4000000000, bytes_accessed=4000000, transcendentals=0
        ),
        name="arrange",
    )(raw)


def project_spans(place, levels, modulation, weight, blocks):
    row = jnp.arange(256)
    perm = (row[:, None] == (2 * (row % 128) + row // 128)[None, :]).astype(bf16)
    smem = pl.BlockSpec(memory_space=pltpu.SMEM)
    vmem = pl.BlockSpec(memory_space=pltpu.VMEM)
    return pl.pallas_call(
        qkv_kernel,
        out_shape=(
            jax.ShapeDtypeStruct((SPANS, ROWS, LANES), bf16),
            jax.ShapeDtypeStruct((SPANS, ROWS, KVW), bf16),
            jax.ShapeDtypeStruct((ROWS, D), bf16),
        ),
        in_specs=[smem, smem] + [vmem] * (3 + SPANS),
        out_specs=(vmem,) * 3,
        scratch_shapes=[pltpu.VMEM((SPANS * ROWS, D), f32)],
        compiler_params=pltpu.CompilerParams(vmem_limit_bytes=VMEM_LIMIT),
        cost_estimate=pl.CostEstimate(
            flops=2 * SPANS * ROWS * D * 640, bytes_accessed=4500000, transcendentals=0
        ),
        name="qkv",
    )(place, levels, modulation, perm, weight, *blocks)


def split_bf16(value, count):
    parts = []
    for _ in range(count):
        part = value.astype(bf16).astype(f32)
        parts.append(part)
        value = value - part
    return parts


def pack(heads, tops):
    lane = lax.broadcasted_iota(jnp.int32, (1, LANES), 1)
    merged = jnp.where(lane < HDIM, heads[0], jnp.where(lane < 2 * HDIM, heads[1], heads[2]))
    columns = []
    for head in range(GROUP):
        columns += split_bf16(tops[head], 3)
        columns += split_bf16(heads[head][:, 192:193], 2)
    for index, column in enumerate(columns):
        merged = jnp.where(lane == 192 + index, column, merged)
    return merged


def attend_first_kernel(place, qa, qb, kv, out):
    lane = lax.broadcasted_iota(jnp.int32, (1, LANES), 1)
    rows = 2 * ROWS
    both = jnp.concatenate([qa[0].astype(f32), qb[0].astype(f32)], axis=0)
    block = kv[:, 0].astype(f32).reshape(kv.shape[0] * ROWS, KVW)
    values = jnp.where(lane // HDIM == 3, 1.0, block[:, :LANES]).astype(bf16)
    keys = block[:, KVW - LANES :].astype(bf16)
    heads, tops = [], []
    for head in range(GROUP):
        query = jnp.where(lane // HDIM == head + 1, both, 0.0).astype(bf16)
        scores = lax.dot_general(
            query, keys, (((1,), (1,)), ((), ())), preferred_element_type=f32
        )
        top = jnp.max(scores, axis=1, keepdims=True)
        probs = jnp.exp(scores - top).astype(bf16)
        heads.append(jnp.dot(probs, values, preferred_element_type=f32))
        tops.append(top)
    merged = pack(heads, tops)
    mine = place[1]
    for span in range(SPANS):
        out[span, mine] = merged[:ROWS].astype(bf16)
        out[span, 1 - mine] = merged[ROWS:].astype(bf16)


def attend_first(place, qa, qb, kv):
    head = pl.BlockSpec((1, ROWS, LANES), lambda i: (0, 0, 0))
    return pl.pallas_call(
        attend_first_kernel,
        grid=(1,),
        out_shape=jax.ShapeDtypeStruct((SPANS, 2, ROWS, LANES), bf16),
        in_specs=[
            pl.BlockSpec(memory_space=pltpu.SMEM),
            head,
            head,
            pl.BlockSpec((kv.shape[0], 1, ROWS, KVW), lambda i: (0, 0, 0, 0)),
        ],
        out_specs=pl.BlockSpec((SPANS, 2, ROWS, LANES), lambda i: (0, 0, 0, 0)),
        compiler_params=pltpu.CompilerParams(vmem_limit_bytes=VMEM_LIMIT),
        cost_estimate=pl.CostEstimate(
            flops=600000000, bytes_accessed=2000000, transcendentals=500000
        ),
        name="attend_first",
    )(place, qa, qb, kv)


def attend_kernel(
    place, mask, qa, qb, kv, out, pairs, queries, keys, values, s0, s1, p0, p1, r0, r1, acc, peak
):
    step = pl.program_id(0)
    count = kv.shape[0] * ROWS
    rows = 2 * ROWS
    stack = GROUP * rows
    lane = lax.broadcasted_iota(jnp.int32, (1, LANES), 1)

    @pl.when(step == 0)
    def _():
        for span in range(SPANS):
            both = jnp.concatenate([qa[span].astype(f32), qb[span].astype(f32)], axis=0)
            for head in range(GROUP):
                queries[span, head * rows : (head + 1) * rows, :] = jnp.where(
                    lane // HDIM == head + 1, both, 0.0
                ).astype(bf16)
        queries[SPANS] = jnp.zeros((stack, LANES), bf16)
        acc[...] = jnp.zeros_like(acc)
        peak[...] = jnp.full_like(peak, LOW)
        p0[...] = jnp.zeros_like(p0)
        r0[...] = jnp.zeros_like(r0)

    block = kv[:, 0].astype(f32).reshape(count, KVW)
    values[step] = jnp.where(lane // HDIM == 3, 1.0, block[:, :LANES]).astype(bf16)
    keys[step] = block[:, KVW - LANES :].astype(bf16)

    def put(index, span, key_span):
        pairs[2 * index] = span
        pairs[2 * index + 1] = key_span

    def score(index, scores):
        scores[...] = lax.dot_general(
            queries[pairs[2 * index]],
            keys[pairs[2 * index + 1]],
            (((1,), (1,)), ((), ())),
            preferred_element_type=f32,
        )

    def weigh(index, scores, probs, rescale):
        span = pairs[2 * index]
        old = peak[span, :, 0:1]
        block = scores[...]
        new = jnp.maximum(old, jnp.max(block, axis=1, keepdims=True))
        probs[...] = jnp.exp(block - new).astype(bf16)
        peak[span] = jnp.broadcast_to(new, (stack, 128))
        rescale[...] = jnp.broadcast_to(jnp.exp(old - new), (stack, 128))

    def blend(index, probs, rescale):
        span = pairs[2 * index]
        acc[span] = acc[span] * rescale[:, 0:1] + jnp.dot(
            probs[...], values[pairs[2 * index + 1]], preferred_element_type=f32
        )

    @pl.when(step == SPANS - 1)
    def _():
        put(0, SPANS, 0)

        def scan(at, found):
            span, key_span = at // SPANS, at % SPANS
            seen = mask[span, key_span] > 0

            @pl.when(seen)
            def _():
                put(found, span, key_span)

            return jnp.where(seen, found + 1, found)

        found = lax.fori_loop(0, SPANS * SPANS, scan, jnp.int32(1))
        for extra in range(4):
            put(found + extra, SPANS, 0)
        score(1, s1)

        def both_slots(trip, carry):
            at = 2 * trip + 1
            score(at + 1, s0)
            weigh(at, s1, p1, r1)
            blend(at - 1, p0, r0)
            score(at + 2, s1)
            weigh(at + 1, s0, p0, r0)
            blend(at, p1, r1)
            return carry

        lax.fori_loop(0, (found + 1) // 2, both_slots, 0)

        mine = place[1]
        for span in range(SPANS):
            heads = [acc[span, head * rows : (head + 1) * rows, :] for head in range(GROUP)]
            tops = [peak[span, head * rows : (head + 1) * rows, 0:1] for head in range(GROUP)]
            merged = pack(heads, tops)
            out[span, mine] = merged[:ROWS].astype(bf16)
            out[span, 1 - mine] = merged[ROWS:].astype(bf16)


def attend(place, mask, qa, qb, kv):
    sources = kv.shape[0]
    smem = pl.BlockSpec(memory_space=pltpu.SMEM)
    vmem = pl.BlockSpec(memory_space=pltpu.VMEM)
    stack = 2 * ROWS * GROUP
    count = sources * ROWS
    return pl.pallas_call(
        attend_kernel,
        grid=(SPANS,),
        out_shape=jax.ShapeDtypeStruct((SPANS, 2, ROWS, LANES), bf16),
        in_specs=[
            smem,
            smem,
            vmem,
            vmem,
            pl.BlockSpec((sources, 1, ROWS, KVW), lambda i: (0, i, 0, 0)),
        ],
        out_specs=pl.BlockSpec((SPANS, 2, ROWS, LANES), lambda i: (0, 0, 0, 0)),
        scratch_shapes=[
            pltpu.SMEM((2 * (SPANS * SPANS + 8),), jnp.int32),
            pltpu.VMEM((SPANS + 1, stack, LANES), bf16),
            pltpu.VMEM((SPANS, count, LANES), bf16),
            pltpu.VMEM((SPANS, count, LANES), bf16),
            pltpu.VMEM((stack, count), f32),
            pltpu.VMEM((stack, count), f32),
            pltpu.VMEM((stack, count), bf16),
            pltpu.VMEM((stack, count), bf16),
            pltpu.VMEM((stack, 128), f32),
            pltpu.VMEM((stack, 128), f32),
            pltpu.VMEM((SPANS + 1, stack, LANES), f32),
            pltpu.VMEM((SPANS + 1, stack, 128), f32),
        ],
        compiler_params=pltpu.CompilerParams(
            vmem_limit_bytes=VMEM_LIMIT, dimension_semantics=("arbitrary",)
        ),
        cost_estimate=pl.CostEstimate(
            flops=8000000000, bytes_accessed=8000000, transcendentals=12000000
        ),
        name="attend",
    )(place, mask, qa, qb, kv)


def finish_kernel(place, levels, parts, near, far, tokens, mod, *refs, decode):
    lane = lax.broadcasted_iota(jnp.int32, (HDIM, LANES), 1)
    slot = lax.broadcasted_iota(jnp.int32, (HDIM, LANES), 0)
    head = lane // HDIM
    peaks = jnp.where((slot >= head * 5) & (slot < head * 5 + 3) & (head < 3), 1.0, 0.0).astype(bf16)
    sums = jnp.where((slot >= head * 5 + 3) & (slot < head * 5 + 5) & (head < 3), 1.0, 0.0).astype(
        bf16
    )
    if decode:
        head_full, bias, patches, weight = refs
    else:
        hidden, weight = refs
    total = jnp.zeros((ROWS, D), f32)
    core = place[2]
    for step in range(SPANS):
        group = lax.rem(place[0] - step + SPANS, SPANS)
        weight[step, :96, :] = jnp.where(core == 0, near[step], far[step])
        weight[step, 96:, :] = jnp.where(core == 0, far[step], near[step])
        tops, totals, outs = [], [], []
        for half in range(2):
            part = parts[group * 2 + half]
            tops.append(jnp.dot(part[:, 192:], peaks, preferred_element_type=f32))
            totals.append(jnp.dot(part[:, 192:], sums, preferred_element_type=f32))
            outs.append(part.astype(f32))
        top = jnp.maximum(tops[0], tops[1])
        scale = [jnp.exp(tops[0] - top), jnp.exp(tops[1] - top)]
        blended = (outs[0] * scale[0] + outs[1] * scale[1]) / (
            totals[0] * scale[0] + totals[1] * scale[1]
        )
        total += jnp.dot(
            blended[:, :192].astype(bf16), weight[step], preferred_element_type=f32
        )
    level = levels[0] if decode else levels[place[0]]
    result = (tokens[...].astype(f32) + mod[level, 2:3, :] * total).astype(bf16)
    if decode:
        shaped = normalise(result.astype(f32)) * (1.0 + mod[level, 4:5, :]) + mod[level, 3:4, :]
        patches[...] = (
            jnp.dot(shaped.astype(bf16), head_full[...], preferred_element_type=f32) + bias[...]
        ).astype(bf16)
    else:
        hidden[...] = result


def finish(place, levels, parts, near, far, tokens, modulation, *extra):
    smem = pl.BlockSpec(memory_space=pltpu.SMEM)
    vmem = pl.BlockSpec(memory_space=pltpu.VMEM)
    decode = len(extra) > 0
    return pl.pallas_call(
        functools.partial(finish_kernel, decode=decode),
        out_shape=jax.ShapeDtypeStruct((ROWS, 4 * LCH if decode else D), bf16),
        in_specs=[smem, smem] + [vmem] * (5 + len(extra)),
        out_specs=vmem,
        scratch_shapes=[pltpu.VMEM((SPANS, 192, D), bf16)],
        compiler_params=pltpu.CompilerParams(vmem_limit_bytes=VMEM_LIMIT),
        cost_estimate=pl.CostEstimate(
            flops=2 * ROWS * D * D, bytes_accessed=6000000, transcendentals=0
        ),
        name="finish_first" if decode else "finish",
    )(place, levels, parts, near, far, tokens, modulation, *extra)


def per_device(
    tokens,
    noise_steps,
    span_mask,
    modulation,
    qkv_weight,
    out_weight,
    head_weight,
    head_bias,
    frame_cache,
    conv_weight,
    conv_bias,
):
    span = lax.axis_index(SPAN)
    yhi = lax.axis_index("yhi")
    core = lax.axis_index("core")
    place = jnp.stack([span, yhi, core]).astype(jnp.int32)
    own = tokens[0]

    beside = shift(own, "ylo", 2, 1)
    lower, upper = shift(own, "x", 4, 1), shift(own, "x", 4, -1)
    lower_beside, upper_beside = shift(beside, "x", 4, 1), shift(beside, "x", 4, -1)
    across, across_beside = shift(lower, "x", 4, 1), shift(upper_beside, "x", 4, -1)
    blocks = [own, beside, lower, upper, lower_beside, upper_beside, across, across_beside]

    weight = arrange(qkv_weight)
    q_own, kv_own, first = project_spans(place, noise_steps, modulation, weight, blocks)

    kv = lax.all_gather(kv_own, ("z", "core"))
    q_other = shift(q_own, "yhi", 2, 1)

    half = lax.dynamic_slice_in_dim(out_weight, core * 96, 96, 0)
    half, _ = lax.optimization_barrier((half, q_own))
    near = jnp.stack([half] + [shift(half, SPAN, SPANS, step) for step in range(1, SPANS)])
    far = shift(near, "core", 2, 1)

    first_partial = attend_first(place, q_own, q_other, kv)
    first_parts = lax.all_to_all(
        first_partial.reshape(2 * SPANS, ROWS, LANES), SPAN + ("yhi",), 0, 0
    )
    partial = attend(place, span_mask, q_own, q_other, kv)
    parts = lax.all_to_all(partial.reshape(2 * SPANS, ROWS, LANES), SPAN + ("yhi",), 0, 0)
    first_parts, _ = lax.optimization_barrier((first_parts, partial))
    patches = finish(
        place,
        noise_steps,
        first_parts,
        near,
        far,
        first,
        modulation,
        head_weight.reshape(D, 4 * LCH),
        head_bias[None, :],
    )
    hidden = finish(place, noise_steps, parts, near, far, own, modulation)

    latent = patches.reshape(LF, TCOL, 2, 2, LCH)
    latent = jnp.transpose(latent, (0, 2, 1, 3, 4)).reshape(LF, 2, 2 * TCOL, LCH)
    frames = jnp.concatenate([frame_cache, latent], axis=0)
    up = [(i, i + 1) for i in range(31)]
    down = [(i + 1, i) for i in range(31)]
    above = lax.ppermute(frames[:, 1:2], TILE, up)
    below = lax.ppermute(frames[:, 0:1], TILE, down)
    padded = jnp.concatenate([above, frames, below], axis=1)
    padded = jnp.pad(padded, ((0, 0), (0, 0), (1, 1), (0, 0)))
    mine = lax.dynamic_slice_in_dim(padded, span * 6, 8, axis=2)
    product = lax.conv_general_dilated(
        mine[None],
        conv_weight.reshape(3, 3, 3, LCH, VCH),
        (1, 1, 1),
        "VALID",
        dimension_numbers=("NDHWC", "DHWIO", "NDHWC"),
        preferred_element_type=f32,
    )
    decoded = (product[0] + conv_bias).astype(bf16)
    return (hidden[None], decoded)


def solution(mesh):
    fine = Mesh(mesh.devices.reshape(4, 2, 8, 2, 2), SPAN + TILE)
    in_specs = (
        P(SPAN, TILE, None),
        P(),
        P(),
        P(),
        P(None, SPAN),
        P(SPAN, None),
        P(),
        P(),
        P(None, TILE, None, None),
        P(),
        P(),
    )
    out_specs = (P(SPAN, TILE, None), P(None, TILE, SPAN, None))
    return jax.shard_map(
        per_device, mesh=fine, in_specs=in_specs, out_specs=out_specs, check_vma=False
    )
```

```python
import functools

import jax
import jax.numpy as jnp
from jax import lax
from jax.experimental import pallas as pl
from jax.experimental.pallas import tpu as pltpu
from jax.sharding import Mesh
from jax.sharding import PartitionSpec as P

HDIM = 64
LCH = 16
LF = 3
TCOL = 24
D = 1536
SPANS = 8
ROWS = 72
VCH = 384
GROUP = 3
LANES = 256
KVW = 384
EPS = 1e-06
LOW = -1e30
SPAN = ("x", "ylo")
TILE = ("z", "yhi", "core")
VMEM_LIMIT = 48 * 1024 * 1024
OFFSETS = ((0, 0), (0, 1), (3, 0), (1, 0), (3, 1), (1, 1), (2, 0), (2, 1))

bf16 = jnp.bfloat16
f32 = jnp.float32


def shift(block, axis, count, step):
    return lax.ppermute(block, axis, [(i, (i + step) % count) for i in range(count)])


def normalise(values):
    centred = values - jnp.mean(values, axis=-1, keepdims=True)
    spread = jnp.mean(centred * centred, axis=-1, keepdims=True)
    return centred * lax.rsqrt(spread + EPS)


def qkv_kernel(place, levels, mod, perm, weight, *refs):
    tokens = refs[:SPANS]
    q_ref, kv_ref, first_ref, normed = refs[SPANS:]
    me = place[0]
    for step in range(SPANS):
        span = lax.rem(me // 2 + OFFSETS[step][0], 4) * 2 + lax.rem(me + OFFSETS[step][1], 2)
        level = levels[span]
        values = normalise(tokens[step][...].astype(f32))
        values = values * (1.0 + mod[level, 1:2, :]) + mod[level, 0:1, :]
        normed[step * ROWS : (step + 1) * ROWS, :] = values
    total = jnp.zeros((SPANS * ROWS, LANES + KVW), f32)
    for block in range(D // 256):
        part = normed[:, block * 256 : (block + 1) * 256].astype(bf16)
        part = jnp.dot(part, perm[...], preferred_element_type=f32).astype(bf16)
        total += jnp.dot(
            part, weight[block * 256 : (block + 1) * 256, :], preferred_element_type=f32
        )
    for step in range(SPANS):
        span = lax.rem(me // 2 + OFFSETS[step][0], 4) * 2 + lax.rem(me + OFFSETS[step][1], 2)
        rows = total[step * ROWS : (step + 1) * ROWS, :].astype(bf16)
        q_ref[span] = rows[:, :LANES] * jnp.asarray(HDIM**-0.5, bf16)
        kv_ref[span] = rows[:, LANES:]

        @pl.when(span == 0)
        def _():
            first_ref[...] = tokens[step][...]


def arrange_kernel(raw, out):
    width = LANES + KVW
    row = lax.broadcasted_iota(jnp.int32, (256, width), 0)
    col = lax.broadcasted_iota(jnp.int32, (256, width), 1) - HDIM
    kind = col // (GROUP * HDIM)
    head = (col % (GROUP * HDIM)) // HDIM
    source = jnp.where(kind == 0, 0, 3 - kind) * HDIM + col % HDIM
    for parity in range(2):
        total = jnp.zeros((D // 2, width), f32)
        for group in range(GROUP):
            begin = group * 2 * KVW // 2 + parity * 128
            wanted = (row == source + parity * HDIM) & (head == group) & (col >= 0)
            total += jnp.dot(
                raw[:, begin : begin + 256],
                jnp.where(wanted, 1.0, 0.0).astype(bf16),
                preferred_element_type=f32,
            )
        for block in range(D // 256):
            out[block * 256 + parity * 128 : block * 256 + parity * 128 + 128, :] = total[
                block * 128 : (block + 1) * 128
            ].astype(bf16)


def arrange(raw):
    vmem = pl.BlockSpec(memory_space=pltpu.VMEM)
    return pl.pallas_call(
        arrange_kernel,
        out_shape=jax.ShapeDtypeStruct((D, LANES + KVW), bf16),
        in_specs=[vmem],
        out_specs=vmem,
        compiler_params=pltpu.CompilerParams(vmem_limit_bytes=VMEM_LIMIT),
        cost_estimate=pl.CostEstimate(
            flops=4000000000, bytes_accessed=4000000, transcendentals=0
        ),
        name="arrange",
    )(raw)


def project_spans(place, levels, modulation, weight, blocks):
    row = jnp.arange(256)
    perm = (row[:, None] == (2 * (row % 128) + row // 128)[None, :]).astype(bf16)
    smem = pl.BlockSpec(memory_space=pltpu.SMEM)
    vmem = pl.BlockSpec(memory_space=pltpu.VMEM)
    return pl.pallas_call(
        qkv_kernel,
        out_shape=(
            jax.ShapeDtypeStruct((SPANS, ROWS, LANES), bf16),
            jax.ShapeDtypeStruct((SPANS, ROWS, KVW), bf16),
            jax.ShapeDtypeStruct((ROWS, D), bf16),
        ),
        in_specs=[smem, smem] + [vmem] * (3 + SPANS),
        out_specs=(vmem,) * 3,
        scratch_shapes=[pltpu.VMEM((SPANS * ROWS, D), f32)],
        compiler_params=pltpu.CompilerParams(vmem_limit_bytes=VMEM_LIMIT),
        cost_estimate=pl.CostEstimate(
            flops=2 * SPANS * ROWS * D * 640, bytes_accessed=4500000, transcendentals=0
        ),
        name="qkv",
    )(place, levels, modulation, perm, weight, *blocks)


def split_bf16(value, count):
    parts = []
    for _ in range(count):
        part = value.astype(bf16).astype(f32)
        parts.append(part)
        value = value - part
    return parts


def pack(heads, tops):
    lane = lax.broadcasted_iota(jnp.int32, (1, LANES), 1)
    merged = jnp.where(lane < HDIM, heads[0], jnp.where(lane < 2 * HDIM, heads[1], heads[2]))
    columns = []
    for head in range(GROUP):
        columns += split_bf16(tops[head], 3)
        columns += split_bf16(heads[head][:, 192:193], 2)
    for index, column in enumerate(columns):
        merged = jnp.where(lane == 192 + index, column, merged)
    return merged


def attend_first_kernel(place, qa, qb, kv, out):
    lane = lax.broadcasted_iota(jnp.int32, (1, LANES), 1)
    rows = 2 * ROWS
    both = jnp.concatenate([qa[0].astype(f32), qb[0].astype(f32)], axis=0)
    block = kv[:, 0].astype(f32).reshape(kv.shape[0] * ROWS, KVW)
    values = jnp.where(lane // HDIM == 3, 1.0, block[:, :LANES]).astype(bf16)
    keys = block[:, KVW - LANES :].astype(bf16)
    heads, tops = [], []
    for head in range(GROUP):
        query = jnp.where(lane // HDIM == head + 1, both, 0.0).astype(bf16)
        scores = lax.dot_general(
            query, keys, (((1,), (1,)), ((), ())), preferred_element_type=f32
        )
        top = jnp.max(scores, axis=1, keepdims=True)
        probs = jnp.exp(scores - top).astype(bf16)
        heads.append(jnp.dot(probs, values, preferred_element_type=f32))
        tops.append(top)
    merged = pack(heads, tops)
    mine = place[1]
    for span in range(SPANS):
        out[span, mine] = merged[:ROWS].astype(bf16)
        out[span, 1 - mine] = merged[ROWS:].astype(bf16)


def attend_first(place, qa, qb, kv):
    head = pl.BlockSpec((1, ROWS, LANES), lambda i: (0, 0, 0))
    return pl.pallas_call(
        attend_first_kernel,
        grid=(1,),
        out_shape=jax.ShapeDtypeStruct((SPANS, 2, ROWS, LANES), bf16),
        in_specs=[
            pl.BlockSpec(memory_space=pltpu.SMEM),
            head,
            head,
            pl.BlockSpec((kv.shape[0], 1, ROWS, KVW), lambda i: (0, 0, 0, 0)),
        ],
        out_specs=pl.BlockSpec((SPANS, 2, ROWS, LANES), lambda i: (0, 0, 0, 0)),
        compiler_params=pltpu.CompilerParams(vmem_limit_bytes=VMEM_LIMIT),
        cost_estimate=pl.CostEstimate(
            flops=600000000, bytes_accessed=2000000, transcendentals=500000
        ),
        name="attend_first",
    )(place, qa, qb, kv)


def attend_kernel(
    place, mask, qa, qb, kv, out, pairs, queries, keys, values, s0, s1, p0, p1, r0, r1, acc, peak
):
    step = pl.program_id(0)
    count = kv.shape[0] * ROWS
    rows = 2 * ROWS
    stack = GROUP * rows
    lane = lax.broadcasted_iota(jnp.int32, (1, LANES), 1)

    @pl.when(step == 0)
    def _():
        for span in range(SPANS):
            both = jnp.concatenate([qa[span].astype(f32), qb[span].astype(f32)], axis=0)
            for head in range(GROUP):
                queries[span, head * rows : (head + 1) * rows, :] = jnp.where(
                    lane // HDIM == head + 1, both, 0.0
                ).astype(bf16)
        queries[SPANS] = jnp.zeros((stack, LANES), bf16)
        acc[...] = jnp.zeros_like(acc)
        peak[...] = jnp.full_like(peak, LOW)
        p0[...] = jnp.zeros_like(p0)
        r0[...] = jnp.zeros_like(r0)

    block = kv[:, 0].astype(f32).reshape(count, KVW)
    values[step] = jnp.where(lane // HDIM == 3, 1.0, block[:, :LANES]).astype(bf16)
    keys[step] = block[:, KVW - LANES :].astype(bf16)

    def put(index, span, key_span):
        pairs[2 * index] = span
        pairs[2 * index + 1] = key_span

    def score(index, scores):
        scores[...] = lax.dot_general(
            queries[pairs[2 * index]],
            keys[pairs[2 * index + 1]],
            (((1,), (1,)), ((), ())),
            preferred_element_type=f32,
        )

    def weigh(index, scores, probs, rescale):
        span = pairs[2 * index]
        old = peak[span, :, 0:1]
        block = scores[...]
        new = jnp.maximum(old, jnp.max(block, axis=1, keepdims=True))
        probs[...] = jnp.exp(block - new).astype(bf16)
        peak[span] = jnp.broadcast_to(new, (stack, 128))
        rescale[...] = jnp.broadcast_to(jnp.exp(old - new), (stack, 128))

    def blend(index, probs, rescale):
        span = pairs[2 * index]
        acc[span] = acc[span] * rescale[:, 0:1] + jnp.dot(
            probs[...], values[pairs[2 * index + 1]], preferred_element_type=f32
        )

    @pl.when(step == SPANS - 1)
    def _():
        put(0, SPANS, 0)

        def scan(at, found):
            span, key_span = at // SPANS, at % SPANS
            seen = mask[span, key_span] > 0

            @pl.when(seen)
            def _():
                put(found, span, key_span)

            return jnp.where(seen, found + 1, found)

        found = lax.fori_loop(0, SPANS * SPANS, scan, jnp.int32(1))
        for extra in range(4):
            put(found + extra, SPANS, 0)
        score(1, s1)

        def both_slots(trip, carry):
            at = 2 * trip + 1
            score(at + 1, s0)
            weigh(at, s1, p1, r1)
            blend(at - 1, p0, r0)
            score(at + 2, s1)
            weigh(at + 1, s0, p0, r0)
            blend(at, p1, r1)
            return carry

        lax.fori_loop(0, (found + 1) // 2, both_slots, 0)

        mine = place[1]
        for span in range(SPANS):
            heads = [acc[span, head * rows : (head + 1) * rows, :] for head in range(GROUP)]
            tops = [peak[span, head * rows : (head + 1) * rows, 0:1] for head in range(GROUP)]
            merged = pack(heads, tops)
            out[span, mine] = merged[:ROWS].astype(bf16)
            out[span, 1 - mine] = merged[ROWS:].astype(bf16)


def attend(place, mask, qa, qb, kv):
    sources = kv.shape[0]
    smem = pl.BlockSpec(memory_space=pltpu.SMEM)
    vmem = pl.BlockSpec(memory_space=pltpu.VMEM)
    stack = 2 * ROWS * GROUP
    count = sources * ROWS
    return pl.pallas_call(
        attend_kernel,
        grid=(SPANS,),
        out_shape=jax.ShapeDtypeStruct((SPANS, 2, ROWS, LANES), bf16),
        in_specs=[
            smem,
            smem,
            vmem,
            vmem,
            pl.BlockSpec((sources, 1, ROWS, KVW), lambda i: (0, i, 0, 0)),
        ],
        out_specs=pl.BlockSpec((SPANS, 2, ROWS, LANES), lambda i: (0, 0, 0, 0)),
        scratch_shapes=[
            pltpu.SMEM((2 * (SPANS * SPANS + 8),), jnp.int32),
            pltpu.VMEM((SPANS + 1, stack, LANES), bf16),
            pltpu.VMEM((SPANS, count, LANES), bf16),
            pltpu.VMEM((SPANS, count, LANES), bf16),
            pltpu.VMEM((stack, count), f32),
            pltpu.VMEM((stack, count), f32),
            pltpu.VMEM((stack, count), bf16),
            pltpu.VMEM((stack, count), bf16),
            pltpu.VMEM((stack, 128), f32),
            pltpu.VMEM((stack, 128), f32),
            pltpu.VMEM((SPANS + 1, stack, LANES), f32),
            pltpu.VMEM((SPANS + 1, stack, 128), f32),
        ],
        compiler_params=pltpu.CompilerParams(
            vmem_limit_bytes=VMEM_LIMIT, dimension_semantics=("arbitrary",)
        ),
        cost_estimate=pl.CostEstimate(
            flops=8000000000, bytes_accessed=8000000, transcendentals=12000000
        ),
        name="attend",
    )(place, mask, qa, qb, kv)


def finish_kernel(place, levels, parts, near, far, tokens, mod, *refs, decode):
    lane = lax.broadcasted_iota(jnp.int32, (HDIM, LANES), 1)
    slot = lax.broadcasted_iota(jnp.int32, (HDIM, LANES), 0)
    head = lane // HDIM
    peaks = jnp.where((slot >= head * 5) & (slot < head * 5 + 3) & (head < 3), 1.0, 0.0).astype(bf16)
    sums = jnp.where((slot >= head * 5 + 3) & (slot < head * 5 + 5) & (head < 3), 1.0, 0.0).astype(
        bf16
    )
    if decode:
        head_full, bias, patches, weight = refs
    else:
        hidden, weight = refs
    total = jnp.zeros((ROWS, D), f32)
    core = place[2]
    for step in range(SPANS):
        group = lax.rem(place[0] - step + SPANS, SPANS)
        weight[step, :96, :] = jnp.where(core == 0, near[step], far[step])
        weight[step, 96:, :] = jnp.where(core == 0, far[step], near[step])
        tops, totals, outs = [], [], []
        for half in range(2):
            part = parts[group * 2 + half]
            tops.append(jnp.dot(part[:, 192:], peaks, preferred_element_type=f32))
            totals.append(jnp.dot(part[:, 192:], sums, preferred_element_type=f32))
            outs.append(part.astype(f32))
        top = jnp.maximum(tops[0], tops[1])
        scale = [jnp.exp(tops[0] - top), jnp.exp(tops[1] - top)]
        blended = (outs[0] * scale[0] + outs[1] * scale[1]) / (
            totals[0] * scale[0] + totals[1] * scale[1]
        )
        total += jnp.dot(
            blended[:, :192].astype(bf16), weight[step], preferred_element_type=f32
        )
    level = levels[0] if decode else levels[place[0]]
    result = (tokens[...].astype(f32) + mod[level, 2:3, :] * total).astype(bf16)
    if decode:
        shaped = normalise(result.astype(f32)) * (1.0 + mod[level, 4:5, :]) + mod[level, 3:4, :]
        patches[...] = (
            jnp.dot(shaped.astype(bf16), head_full[...], preferred_element_type=f32) + bias[...]
        ).astype(bf16)
    else:
        hidden[...] = result


def finish(place, levels, parts, near, far, tokens, modulation, *extra):
    smem = pl.BlockSpec(memory_space=pltpu.SMEM)
    vmem = pl.BlockSpec(memory_space=pltpu.VMEM)
    decode = len(extra) > 0
    return pl.pallas_call(
        functools.partial(finish_kernel, decode=decode),
        out_shape=jax.ShapeDtypeStruct((ROWS, 4 * LCH if decode else D), bf16),
        in_specs=[smem, smem] + [vmem] * (5 + len(extra)),
        out_specs=vmem,
        scratch_shapes=[pltpu.VMEM((SPANS, 192, D), bf16)],
        compiler_params=pltpu.CompilerParams(vmem_limit_bytes=VMEM_LIMIT),
        cost_estimate=pl.CostEstimate(
            flops=2 * ROWS * D * D, bytes_accessed=6000000, transcendentals=0
        ),
        name="finish_first" if decode else "finish",
    )(place, levels, parts, near, far, tokens, modulation, *extra)


def per_device(
    tokens,
    noise_steps,
    span_mask,
    modulation,
    qkv_weight,
    out_weight,
    head_weight,
    head_bias,
    frame_cache,
    conv_weight,
    conv_bias,
):
    span = lax.axis_index(SPAN)
    yhi = lax.axis_index("yhi")
    core = lax.axis_index("core")
    place = jnp.stack([span, yhi, core]).astype(jnp.int32)
    own = tokens[0]

    beside = shift(own, "ylo", 2, 1)
    lower, upper = shift(own, "x", 4, 1), shift(own, "x", 4, -1)
    lower_beside, upper_beside = shift(beside, "x", 4, 1), shift(beside, "x", 4, -1)
    across, across_beside = shift(lower, "x", 4, 1), shift(upper_beside, "x", 4, -1)
    blocks = [own, beside, lower, upper, lower_beside, upper_beside, across, across_beside]

    weight = arrange(qkv_weight)
    q_own, kv_own, first = project_spans(place, noise_steps, modulation, weight, blocks)

    kv = lax.all_gather(kv_own, ("z", "core"))
    q_other = shift(q_own, "yhi", 2, 1)

    half = lax.dynamic_slice_in_dim(out_weight, core * 96, 96, 0)
    half, _ = lax.optimization_barrier((half, q_own))
    near = jnp.stack([half] + [shift(half, SPAN, SPANS, step) for step in range(1, SPANS)])
    far = shift(near, "core", 2, 1)

    first_partial = attend_first(place, q_own, q_other, kv)
    first_parts = lax.all_to_all(
        first_partial.reshape(2 * SPANS, ROWS, LANES), SPAN + ("yhi",), 0, 0
    )
    partial = attend(place, span_mask, q_own, q_other, kv)
    parts = lax.all_to_all(partial.reshape(2 * SPANS, ROWS, LANES), SPAN + ("yhi",), 0, 0)
    first_parts, _ = lax.optimization_barrier((first_parts, partial))
    patches = finish(
        place,
        noise_steps,
        first_parts,
        near,
        far,
        first,
        modulation,
        head_weight.reshape(D, 4 * LCH),
        head_bias[None, :],
    )
    latent = patches.reshape(LF, TCOL, 2, 2, LCH)
    latent = jnp.transpose(latent, (0, 2, 1, 3, 4)).reshape(LF, 2, 2 * TCOL, LCH)
    frames = jnp.concatenate([frame_cache, latent], axis=0)
    up = [(i, i + 1) for i in range(31)]
    down = [(i + 1, i) for i in range(31)]
    above = lax.ppermute(frames[:, 1:2], TILE, up)
    below = lax.ppermute(frames[:, 0:1], TILE, down)
    padded = jnp.concatenate([above, frames, below], axis=1)
    padded = jnp.pad(padded, ((0, 0), (0, 0), (1, 1), (0, 0)))
    mine = lax.dynamic_slice_in_dim(padded, span * 6, 8, axis=2)
    product = lax.conv_general_dilated(
        mine[None],
        conv_weight.reshape(3, 3, 3, LCH, VCH),
        (1, 1, 1),
        "VALID",
        dimension_numbers=("NDHWC", "DHWIO", "NDHWC"),
        preferred_element_type=f32,
    )
    decoded = (product[0] + conv_bias).astype(bf16)
    parts, decoded = lax.optimization_barrier((parts, decoded))
    hidden = finish(place, noise_steps, parts, near, far, own, modulation)
    return (hidden[None], decoded)


def solution(mesh):
    fine = Mesh(mesh.devices.reshape(4, 2, 8, 2, 2), SPAN + TILE)
    in_specs = (
        P(SPAN, TILE, None),
        P(),
        P(),
        P(),
        P(None, SPAN),
        P(SPAN, None),
        P(),
        P(),
        P(None, TILE, None, None),
        P(),
        P(),
    )
    out_specs = (P(SPAN, TILE, None), P(None, TILE, SPAN, None))
    return jax.shard_map(
        per_device, mesh=fine, in_specs=in_specs, out_specs=out_specs, check_vma=False
    )
```
